256 devices in a mesh: ray: 64 (over x, z, core), row: 4 (over y).
Axes of the slice: x: 4, y: 4, z: 8, core: 2. Of those that a mesh axis runs over, the one named last changes fastest.
Arguments:
- density: float32 [2048, 64, 1024], P('ray', 'row'), may hold values from 0.2 to 5
- light_dir: float32 [3], replicated, may hold values from -1 to 1
- colour_tint: float32 [3], replicated, may hold values from 0.5 to 2
- cotangent: float32 [3, 64, 1024], P(None, 'row'), may hold values from -6 to 6
Outputs:
- dens_grad: float32 [2048, 64, 1024], P('ray', 'row')
The draws below stay inside these ranges and needn't reach their ends.
All inputs are finite; a program needn't handle non-finite values.
Results may differ from the reference program's by a relative error of at most 0.0003.
Values sent between devices are 32-bit elements; how exact they have to be, the bound alone decides.
No kernel may reach another device: no remote copies, remote signals or barrier semaphores. Data moves between devices by JAX's collectives and lax.ppermute only.
A program may use at most 128 MiB of HBM per device.

```python
import math
import jax
import jax.numpy as jnp
from jax import lax

NCOL = 1024
NDEP = 2048
NROW = 64


def steps_of(rng, dims, cuts, least, largest):
    loudness = 1.0
    for axis_at, shards_of in cuts:
        steps = jax.random.uniform(jax.random.fold_in(jax.random.fold_in(rng, 6), axis_at), (shards_of,), jnp.float32, least / len(cuts), largest / len(cuts))
        loudness = loudness * jnp.repeat(jnp.exp(steps), dims[axis_at] // shards_of).reshape((-1,) + (1,) * (len(dims) - 1 - axis_at))
    return loudness


def bell_draw(key, dims, width, limit, split=(), kind=jnp.bfloat16):
    values = jax.random.normal(key, dims, jnp.float32) * width
    if len(split) > 0:
        values = steps_of(key, dims, split, -0.22, 0.18) * values
    return jnp.clip(values, min=-limit, max=limit).astype(kind)


def setup_inputs(seed: int = 0) -> dict:
    key_list = jax.random.split(jax.random.key(seed), 5)
    density = jnp.clip(jnp.exp(math.log(5.0) - 3.218876 * jax.random.uniform(key_list[0], (NDEP, NROW, NCOL), jnp.float32) ** steps_of(key_list[0], (NDEP, NROW, NCOL), ((0, 64), (1, 4)), -0.2, 0.2)), 0.2, 5.0)
    light_dir = jnp.clip(jax.random.uniform(key_list[1], (3,), jnp.float32, -1.0, 1.0), -1.0, 1.0)
    colour_tint = jnp.clip(jnp.exp(jax.random.uniform(key_list[2], (3,), jnp.float32, math.log(0.5), math.log(2.0))), 0.5, 2.0)
    cotangent = bell_draw(key_list[3], (3, NROW, NCOL), 1.0, 6.0, ((1, 4),), jnp.float32)
    return {"density": density, "light_dir": light_dir, "colour_tint": colour_tint, "cotangent": cotangent}


EXTINCTION = 0.7

def window_objective(window, cot_rows, light_dir, colour_tint):
    padded = jnp.pad(window, ((1, 1), (0, 0), (1, 1)))
    grad_x = (padded[2:, 1:-1, 1:-1] - padded[:-2, 1:-1, 1:-1]) * 0.5
    grad_y = (padded[1:-1, 2:, 1:-1] - padded[1:-1, :-2, 1:-1]) * 0.5
    grad_z = (padded[1:-1, 1:-1, 2:] - padded[1:-1, 1:-1, :-2]) * 0.5
    centre = window[:, 1:-1]
    radius = jnp.sqrt(1.0 + grad_x * grad_x + grad_y * grad_y + grad_z * grad_z)
    lit = light_dir[0] * grad_x + light_dir[1] * grad_y + light_dir[2] * grad_z
    shading = 0.5 + 0.5 * lit / radius
    optical = centre * (EXTINCTION / NDEP)
    transmit = jnp.exp(-(jnp.cumsum(optical, axis=0) - optical))
    weight = transmit * (1.0 - jnp.exp(-optical)) * centre * shading
    pixels = lax.optimization_barrier(jnp.sum(weight, axis=0))
    return jnp.sum(cot_rows * colour_tint[:, None, None] * pixels[None])

def reference(density, light_dir, colour_tint, cotangent):
    padded_rows = jnp.pad(density, ((0, 0), (2, 2), (0, 0)))
    padded_cot = jnp.pad(cotangent, ((0, 0), (1, 1), (0, 0)))
    gradient_fn = jax.grad(window_objective)

    def one_block(row_block):
        first_row = (row_block * 8).astype(jnp.int32)
        anchor = jnp.zeros((), jnp.int32)
        window = lax.dynamic_slice(padded_rows, (anchor, first_row, anchor), (NDEP, 12, NCOL))
        cot_rows = lax.dynamic_slice(padded_cot, (anchor, first_row, anchor), (3, 10, NCOL))
        return gradient_fn(window, cot_rows, light_dir, colour_tint)[:, 2:10]
    blocks = lax.map(one_block, jnp.arange(NROW // 8, dtype=jnp.int32))
    stacked = jnp.moveaxis(blocks, 0, 1).reshape(NDEP, NROW, NCOL)
    return stacked * float(NDEP)
```

```python
import functools

import jax
import jax.numpy as jnp
from jax import lax
from jax.experimental import pallas as pl
from jax.experimental.pallas import tpu as pltpu
from jax.sharding import Mesh
from jax.sharding import PartitionSpec as P

RAY = ("ray_0", "ray_1", "ray_2")
EXTINCTION = 0.7
LANES = 128
BLOCK = 8
VM = pl.BlockSpec(memory_space=pltpu.VMEM)
SM = pl.BlockSpec(memory_space=pltpu.SMEM)
HBM = pl.BlockSpec(memory_space=pltpu.HBM)


def sds(*shape):
    return jax.ShapeDtypeStruct(shape, jnp.float32)


def col(c):
    return pl.ds(c * LANES, LANES)


def half(h):
    return pl.ds(h * 8, 8)


def ids():
    lane = lax.broadcasted_iota(jnp.int32, (8, LANES), 1)
    sub = lax.broadcasted_iota(jnp.int32, (8, LANES), 0)
    return lane == 0, lane == LANES - 1, sub == 0, sub == 7


def wide(row):
    return jnp.broadcast_to(row, (8, LANES))


def col_neighbours(tiles, first, last):
    right = [pltpu.roll(t, 1, 1) for t in tiles]
    left = [pltpu.roll(t, LANES - 1, 1) for t in tiles]
    zero = jnp.zeros((8, LANES), jnp.float32)
    n = len(tiles)
    before = [jnp.where(first, right[c - 1] if c else zero, right[c]) for c in range(n)]
    after = [jnp.where(last, left[c + 1] if c < n - 1 else zero, left[c]) for c in range(n)]
    return before, after


def row_neighbours(top, bottom, above, below, first, last):
    down = [pltpu.roll(t, 1, 0) for t in (top, bottom)]
    up = [pltpu.roll(t, 7, 0) for t in (top, bottom)]
    before = (jnp.where(first, above, down[0]), jnp.where(first, down[0], down[1]))
    after = (jnp.where(last, up[1], up[0]), jnp.where(last, below, up[1]))
    return before, after


def absorbed(optical, terms):
    value = 1.0 - optical * (1.0 / terms)
    for n in range(terms - 1, 1, -1):
        value = 1.0 - optical * (1.0 / n) * value
    return optical * value


def gather_kernel(
    place, tint, dens, cot, held, row_first, row_last, to_near, to_cross, rho, held_cot, sems, cot_sem
):
    ndep, nrow, _ = dens.shape
    core_first = place[0] == 0
    colours = pltpu.make_async_copy(cot, held_cot, cot_sem)
    copies = []
    for b in range(ndep // BLOCK):
        part = pl.ds(b * BLOCK, BLOCK)
        copies.append(pltpu.make_async_copy(dens.at[part], held.at[part], sems.at[b]))
        copies[-1].start()
    colours.start()
    for b, copy in enumerate(copies):
        copy.wait()
        for k in range(b * BLOCK, (b + 1) * BLOCK):
            row_first[k] = held[k, 0:1, :]
            row_last[k] = held[k, nrow - 1 : nrow, :]
    first_layer, last_layer = held[0], held[ndep - 1]
    to_near[...] = jnp.where(core_first, last_layer, first_layer)
    to_cross[...] = jnp.where(core_first, first_layer, last_layer)
    colours.wait()
    rho[...] = held_cot[0] * tint[0] + held_cot[1] * tint[1] + held_cot[2] * tint[2]


def shade(light, mid, before, after, lows, highs, masks):
    lx, ly, lz = light
    first, last, head, tail = masks
    nc = len(mid[0])
    zs = [col_neighbours(mid[h], first, last) for h in range(2)]
    out = [[None] * nc, [None] * nc]
    for c in range(nc):
        ys = row_neighbours(mid[0][c], mid[1][c], lows(c), highs(c), head, tail)
        for h in range(2):
            dx = after(h, c) - before(h, c)
            dy = ys[1][h] - ys[0][h]
            dz = zs[h][1][c] - zs[h][0][c]
            inv = lax.rsqrt(4.0 + dx * dx + dy * dy + dz * dz)
            out[h][c] = dx, dy, dz, inv, (lx * dx + ly * dy + lz * dz) * inv
    return out


def opacity(d, step):
    return d * (step - d * (step**2 / 2 - d * (step**3 / 6)))


def forward_kernel(
    step, place, light, dens, near, cross, low, high, rho,
    packed, ends, trans,
):
    ndep, _, ncol = dens.shape
    nc = ncol // LANES
    lights = light[0], light[1], light[2]
    masks = ids()
    core_first = place[0] == 0
    for c in range(nc):
        for h in range(2):
            trans[half(h), col(c)] = jnp.ones((8, LANES), jnp.float32)
            ends[1, half(h), col(c)] = jnp.zeros((8, LANES), jnp.float32)

    def outer(h, c, lower):
        a, b = near[half(h), col(c)], cross[half(h), col(c)]
        return jnp.where(core_first, b, a) if lower else jnp.where(core_first, a, b)

    def layer(k, before, after):
        mid = [[dens[k, half(h), col(c)] for c in range(nc)] for h in range(2)]
        tiles = shade(
            lights, mid, before, after,
            lambda c: wide(low[k, :, col(c)]), lambda c: wide(high[k, :, col(c)]), masks,
        )
        for c in range(nc):
            for h in range(2):
                d, q = mid[h][c], tiles[h][c][4]
                t = trans[half(h), col(c)]
                w = t * opacity(d, step)
                trans[half(h), col(c)] = t - w
                ends[1, half(h), col(c)] += w * d * (0.5 + 0.5 * q)

    layer(0, lambda h, c: outer(h, c, True), lambda h, c: dens[1, half(h), col(c)])

    @pl.loop(1, ndep - 1)
    def _(k):
        layer(k, lambda h, c: dens[k - 1, half(h), col(c)], lambda h, c: dens[k + 1, half(h), col(c)])

    layer(ndep - 1, lambda h, c: dens[ndep - 2, half(h), col(c)], lambda h, c: outer(h, c, False))

    for c in range(nc):
        for h in range(2):
            ends[0, half(h), col(c)] = trans[half(h), col(c)]
    rims = []
    for rim in (low, high):
        total = rim[0]
        for k in range(1, ndep):
            total = total + rim[k]
        rims.append(1.0 - absorbed(total * step, 7))
    for c in range(nc):
        cs = slice(c * LANES, (c + 1) * LANES)
        for h in range(2):
            t = trans[half(h), col(c)]
            v = ends[1, half(h), col(c)] * rho[half(h), col(c)]
            for b in range(4):
                a = h * 4 + b
                p = a * nc + c
                packed[p, :, 0:128] = t[2 * b : 2 * b + 1]
                packed[p, :, 128:256] = t[2 * b + 1 : 2 * b + 2]
                packed[p, :, 256:384] = rims[0][:, cs] if a < 4 else rims[1][:, cs]
                packed[p, :, 384:512] = v[2 * b : 2 * b + 1]
                packed[p, :, 512:640] = v[2 * b + 1 : 2 * b + 2]


def adjoint_kernel(
    step, depth, place, light, dens, near, cross, low, high, rho, ends,
    part, adj_y, adj_z, to_near, to_cross, y_first, y_last,
    held, xs, parts, ys, zs, trans, colour, in_sems, part_sems, y_sems, z_sems,
):
    ndep, _, ncol = dens.shape
    nc = ncol // LANES
    lx, ly, lz = lights = light[0], light[1], light[2]
    masks = ids()
    core_first = place[0] == 0
    blocks = ndep // BLOCK
    arrivals = []
    for b in range(blocks):
        at = pl.ds(b * BLOCK, BLOCK)
        arrivals.append(
            pltpu.make_async_copy(dens.at[at], held.at[pl.ds(b * BLOCK + 1, BLOCK)], in_sems.at[b])
        )
        arrivals[-1].start()
    for c in range(nc):
        for h in range(2):
            at = (half(h), col(c))
            a, b = near[at], cross[at]
            held[0, half(h), col(c)] = jnp.where(core_first, b, a)
            held[ndep + 1, half(h), col(c)] = jnp.where(core_first, a, b)
            trans[at] = jnp.ones((8, LANES), jnp.float32)
            colour[at] = jnp.zeros((8, LANES), jnp.float32)
            for k in (0, 1):
                xs[k, half(h), col(c)] = jnp.zeros((8, LANES), jnp.float32)
            parts[0, half(h), col(c)] = jnp.zeros((8, LANES), jnp.float32)

    def layer(k):
        mid = [[held[k + 1, half(h), col(c)] for c in range(nc)] for h in range(2)]
        tiles = shade(
            lights, mid,
            lambda h, c: held[k, half(h), col(c)], lambda h, c: held[k + 2, half(h), col(c)],
            lambda c: wide(low[k, :, col(c)]), lambda c: wide(high[k, :, col(c)]), masks,
        )
        for c in range(nc):
            for h in range(2):
                at = (half(h), col(c))
                d = mid[h][c]
                dx, dy, dz, inv, q = tiles[h][c]
                lit = 0.5 + 0.5 * q
                t = trans[at]
                w = t * opacity(d, step)
                t = t - w
                trans[at] = t
                wd = w * d
                e = colour[at] + wd * lit
                colour[at] = e
                r = rho[at] * depth
                glow = r * (w * lit + step * (t * (d * lit) + e))
                s = wd * inv * (0.5 * r)
                m = q * inv
                x = s * (lx - m * dx)
                y = s * (ly - m * dy)
                xs[k + 2, half(h), col(c)] = x
                ys[k, half(h), col(c)] = y
                zs[k, half(h), col(c)] = s * (lz - m * dz)
                parts[k + 1, half(h), col(c)] = glow
                parts[k, half(h), col(c)] += xs[k, half(h), col(c)] - x
                if h == 0:
                    y_first[k, :, col(c)] = y[0:1]
                else:
                    y_last[k, :, col(c)] = y[7:8]

    copies = []

    def send(source, target, start, shift, count, sem):
        copies.append(
            pltpu.make_async_copy(
                source.at[pl.ds(start + shift, count)], target.at[pl.ds(start, count)], sem
            )
        )
        copies[-1].start()

    arrivals[0].wait()
    for b in range(blocks):
        if b < blocks - 1:
            arrivals[b + 1].wait()
        pl.loop(b * BLOCK, (b + 1) * BLOCK)(layer)
        send(ys, adj_y, b * BLOCK, 0, BLOCK, y_sems.at[b])
        send(zs, adj_z, b * BLOCK, 0, BLOCK, z_sems.at[b])
        start = max(b * BLOCK - 1, 0)
        send(parts, part, start, 1, (b + 1) * BLOCK - 1 - start, part_sems.at[b])
    for c in range(nc):
        for h in range(2):
            at = (half(h), col(c))
            parts[ndep, half(h), col(c)] += xs[ndep, half(h), col(c)]
            first_x = xs[2, half(h), col(c)]
            last_x = xs[ndep + 1, half(h), col(c)] / ends[0, half(h), col(c)]
            to_near[at] = jnp.where(core_first, last_x, first_x)
            to_cross[at] = jnp.where(core_first, first_x, last_x)
    send(parts, part, ndep - 1, 1, 1, part_sems.at[blocks])
    for copy in copies:
        copy.wait()


def scan_kernel(packed, out):
    slabs = packed.shape[0]
    front = jnp.ones((1, 384), jnp.float32)
    for m in range(slabs):
        out[m, :, 0:384] = front
        if m < slabs - 1:
            front = front * packed[m, :, 0:384]
    behind = jnp.zeros((1, 256), jnp.float32)
    for m in reversed(range(slabs)):
        out[m, :, 384:640] = behind
        if m:
            behind = behind + out[m, :, 0:256] * packed[m, :, 384:640]


def combine_kernel(
    step, depth, place, scanned, x_near, x_cross, y_low, y_high, rho, ends, part, adj_y, adj_z,
    out, front, base, edge, parts, ys, zs, part_sems, y_sems, z_sems, out_sems,
):
    ndep, _, ncol = part.shape
    nc = ncol // LANES
    first, last, head, tail = ids()
    core_first = place[0] == 0
    blocks = ndep // BLOCK
    arrivals = []
    for b in range(blocks):
        at = pl.ds(b * BLOCK, BLOCK)
        arrivals.append(
            [
                pltpu.make_async_copy(source.at[at], target.at[at], sems.at[b])
                for source, target, sems in ((part, parts, part_sems), (adj_y, ys, y_sems), (adj_z, zs, z_sems))
            ]
        )
        for copy in arrivals[-1]:
            copy.start()
    for c in range(nc):
        for a in range(8):
            p = a * nc + c
            front[2 * a : 2 * a + 1, col(c)] = scanned[p, :, 0:128]
            front[2 * a + 1 : 2 * a + 2, col(c)] = scanned[p, :, 128:256]
            base[2 * a : 2 * a + 1, col(c)] = scanned[p, :, 384:512]
            base[2 * a + 1 : 2 * a + 2, col(c)] = scanned[p, :, 512:640]
        edge[0, :, col(c)] = scanned[c, :, 256:384]
        edge[1, :, col(c)] = scanned[7 * nc + c, :, 256:384]
    for c in range(nc):
        for h in range(2):
            at = (half(h), col(c))
            base[at] = (depth * step) * (base[at] + front[at] * (rho[at] * ends[1, half(h), col(c)]))

    def outer(h, c, lower):
        a, b = x_near[half(h), col(c)], x_cross[half(h), col(c)]
        if lower:
            return jnp.where(core_first, b, a)
        return jnp.where(core_first, a, b) * -ends[0, half(h), col(c)]

    def layer(k, extra=None):
        zt, yt = [[], []], [[], []]
        for h in range(2):
            for c in range(nc):
                f = front[half(h), col(c)]
                zt[h].append(f * zs[k, half(h), col(c)])
                yt[h].append(f * ys[k, half(h), col(c)])
        zn = [col_neighbours(zt[h], first, last) for h in range(2)]
        for c in range(nc):
            lo = wide(edge[0, :, col(c)] * y_low[k, :, col(c)])
            hi = wide(edge[1, :, col(c)] * y_high[k, :, col(c)])
            yn = row_neighbours(yt[0][c], yt[1][c], lo, hi, head, tail)
            for h in range(2):
                at, cell = (half(h), col(c)), (k, half(h), col(c))
                own = parts[cell]
                if extra is not None:
                    own = own + outer(h, c, extra)
                parts[cell] = (front[at] * own - base[at]) + (
                    (yn[0][h] - yn[1][h]) + (zn[h][0][c] - zn[h][1][c])
                )

    copies = []
    for b in range(blocks):
        start, stop = b * BLOCK, (b + 1) * BLOCK
        for copy in arrivals[b]:
            copy.wait()
        if b == 0:
            layer(0, True)
            start = 1
        if stop == ndep:
            stop = ndep - 1
        pl.loop(start, stop)(layer)
        if stop == ndep - 1:
            layer(stop, False)
        at = pl.ds(b * BLOCK, BLOCK)
        copies.append(pltpu.make_async_copy(parts.at[at], out.at[at], out_sems.at[b]))
        copies[-1].start()
    for copy in copies:
        copy.wait()


def params(mib):
    return pltpu.CompilerParams(vmem_limit_bytes=mib << 20)


def cost(flops, nbytes):
    return pl.CostEstimate(flops=flops, bytes_accessed=nbytes, transcendentals=0)


def near_memory(*arrays):
    return [pltpu.with_memory_space_constraint(a, pltpu.VMEM) for a in arrays]


def far_memory(*arrays):
    return [pltpu.with_memory_space_constraint(a, pltpu.HBM) for a in arrays]


def local(density, light_dir, colour_tint, cotangent):
    ndep, nrow, ncol = density.shape
    slabs = lax.axis_size(RAY)
    rows = lax.axis_size("row")
    full_depth = float(ndep * slabs)
    step = EXTINCTION / full_depth
    place = lax.axis_index(RAY[2]).reshape(1).astype(jnp.int32)
    swap = [(0, 1), (1, 0)]
    cross = [(i, i + 1) for i in range(1, slabs - 1, 2)] + [(i + 1, i) for i in range(1, slabs - 1, 2)]
    upward = [(i, i + 1) for i in range(rows - 1)]
    downward = [(i + 1, i) for i in range(rows - 1)]

    def exchange(row_first, row_last, to_near, to_cross):
        return near_memory(
            lax.ppermute(to_near, RAY[2], swap),
            lax.ppermute(to_cross, RAY, cross),
            lax.ppermute(row_last, "row", upward),
            lax.ppermute(row_first, "row", downward),
        )

    def vmem(*shape):
        return pltpu.VMEM(shape, jnp.float32)

    def hbm(*shape):
        return pltpu.HBM(shape, jnp.float32)

    cube, layer, rim = (ndep, nrow, ncol), (nrow, ncol), (ndep, 1, ncol)
    share = (slabs, 1, 5 * LANES)
    blocks = ndep // BLOCK
    cells = ndep * nrow * ncol
    sem = pltpu.SemaphoreType.DMA
    held, row_first, row_last, to_near, to_cross, rho = pl.pallas_call(
        gather_kernel,
        out_shape=(vmem(*cube), vmem(*rim), vmem(*rim), vmem(*layer), vmem(*layer), vmem(*layer)),
        in_specs=[SM, SM, HBM, HBM],
        out_specs=[VM] * 6,
        scratch_shapes=[vmem(*cotangent.shape), sem((blocks,)), sem],
        compiler_params=params(4),
        name="gather",
    )(place, colour_tint, *far_memory(density, cotangent))
    halos = exchange(row_first, row_last, to_near, to_cross)
    packed, ends = pl.pallas_call(
        functools.partial(forward_kernel, step),
        out_shape=(vmem(*share), vmem(2, *layer)),
        in_specs=[SM, SM] + [VM] * 6,
        out_specs=[VM] * 2,
        scratch_shapes=[vmem(*layer)],
        compiler_params=params(4),
        cost_estimate=cost(50 * cells, 4 * cells),
        name="forward",
    )(place, light_dir, held, *halos, rho)

    scanned = lax.all_to_all(packed, RAY, 0, 0)
    part, adj_y, adj_z, to_near, to_cross, y_first, y_last = pl.pallas_call(
        functools.partial(adjoint_kernel, step, full_depth),
        out_shape=(hbm(*cube),) * 3 + (vmem(*layer), vmem(*layer), vmem(*rim), vmem(*rim)),
        in_specs=[SM, SM, HBM] + [VM] * 6,
        out_specs=[HBM] * 3 + [VM] * 4,
        scratch_shapes=[
            vmem(ndep + 2, nrow, ncol),
            vmem(ndep + 2, nrow, ncol),
            vmem(ndep + 1, nrow, ncol),
            vmem(*cube),
            vmem(*cube),
            vmem(*layer),
            vmem(*layer),
            sem((blocks,)),
            sem((blocks + 1,)),
            sem((blocks,)),
            sem((blocks,)),
        ],
        compiler_params=params(16),
        cost_estimate=cost(70 * cells, 16 * cells),
        name="adjoint",
    )(place, light_dir, *far_memory(density), *halos, rho, ends)
    scanned, to_near, to_cross, y_first, y_last = lax.optimization_barrier(
        (scanned, to_near, to_cross, y_first, y_last)
    )
    scanned = pl.pallas_call(
        scan_kernel,
        out_shape=vmem(*share),
        in_specs=[VM],
        out_specs=VM,
        compiler_params=params(4),
        name="scan",
    )(*near_memory(scanned))
    scanned = lax.all_to_all(scanned, RAY, 0, 0)
    rims = exchange(y_first, y_last, to_near, to_cross)
    return pl.pallas_call(
        functools.partial(combine_kernel, step, full_depth),
        out_shape=sds(*cube),
        in_specs=[SM] + [VM] * 7 + [HBM] * 3,
        out_specs=HBM,
        scratch_shapes=[
            vmem(*layer),
            vmem(*layer),
            vmem(2, 1, ncol),
            vmem(*cube),
            vmem(*cube),
            vmem(*cube),
            sem((blocks,)),
            sem((blocks,)),
            sem((blocks,)),
            sem((blocks,)),
        ],
        compiler_params=params(16),
        cost_estimate=cost(12 * cells, 16 * cells),
        name="combine",
    )(place, *near_memory(scanned), *rims, rho, ends, *far_memory(part, adj_y, adj_z))


def solution(mesh):
    torus = Mesh(
        mesh.devices.reshape(4, 8, 2, mesh.shape["row"]), ("ray_0", "ray_1", "ray_2", "row")
    )
    placed = (P(RAY, "row", None), P(), P(), P(None, "row", None))
    return jax.shard_map(
        local, mesh=torus, in_specs=placed, out_specs=P(RAY, "row", None), check_vma=False
    )
```

```python
import functools

import jax
import jax.numpy as jnp
from jax import lax
from jax.experimental import pallas as pl
from jax.experimental.pallas import tpu as pltpu
from jax.sharding import Mesh
from jax.sharding import PartitionSpec as P

RAY = ("ray_0", "ray_1", "ray_2")
EXTINCTION = 0.7
LANES = 128
BLOCK = 8
PIECE = 4
VM = pl.BlockSpec(memory_space=pltpu.VMEM)
SM = pl.BlockSpec(memory_space=pltpu.SMEM)
HBM = pl.BlockSpec(memory_space=pltpu.HBM)


def sds(*shape):
    return jax.ShapeDtypeStruct(shape, jnp.float32)


def col(c):
    return pl.ds(c * LANES, LANES)


def half(h):
    return pl.ds(h * 8, 8)


def ids():
    lane = lax.broadcasted_iota(jnp.int32, (8, LANES), 1)
    sub = lax.broadcasted_iota(jnp.int32, (8, LANES), 0)
    return lane == 0, lane == LANES - 1, sub == 0, sub == 7


def wide(row):
    return jnp.broadcast_to(row, (8, LANES))


def col_neighbours(tiles, first, last):
    right = [pltpu.roll(t, 1, 1) for t in tiles]
    left = [pltpu.roll(t, LANES - 1, 1) for t in tiles]
    zero = jnp.zeros((8, LANES), jnp.float32)
    n = len(tiles)
    before = [jnp.where(first, right[c - 1] if c else zero, right[c]) for c in range(n)]
    after = [jnp.where(last, left[c + 1] if c < n - 1 else zero, left[c]) for c in range(n)]
    return before, after


def row_neighbours(top, bottom, above, below, first, last):
    down = [pltpu.roll(t, 1, 0) for t in (top, bottom)]
    up = [pltpu.roll(t, 7, 0) for t in (top, bottom)]
    before = (jnp.where(first, above, down[0]), jnp.where(first, down[0], down[1]))
    after = (jnp.where(last, up[1], up[0]), jnp.where(last, below, up[1]))
    return before, after


def absorbed(optical, terms):
    value = 1.0 - optical * (1.0 / terms)
    for n in range(terms - 1, 1, -1):
        value = 1.0 - optical * (1.0 / n) * value
    return optical * value


def gather_kernel(place, dens, cot, held, held_cot, row_one, row_two, to_near, to_cross, sems, cot_sem):
    ndep, nrow, _ = dens.shape
    core_first, row_first = place[0] == 0, place[1] == 0
    colours = pltpu.make_async_copy(cot, held_cot, cot_sem)
    copies = []
    for b in range(ndep // PIECE):
        part = pl.ds(b * PIECE, PIECE)
        copies.append(pltpu.make_async_copy(dens.at[part], held.at[part], sems.at[b]))
        copies[-1].start()
    colours.start()
    for b, copy in enumerate(copies):
        copy.wait()
        for k in range(b * PIECE, (b + 1) * PIECE):
            top, bottom = held[k, 0:1, :], held[k, nrow - 1 : nrow, :]
            row_one[k] = jnp.where(row_first, bottom, top)
            row_two[k] = jnp.where(row_first, top, bottom)
    first_layer, last_layer = held[0], held[ndep - 1]
    to_near[...] = jnp.where(core_first, last_layer, first_layer)
    to_cross[...] = jnp.where(core_first, first_layer, last_layer)
    colours.wait()


def facing(place, near, cross, one, two):
    core_first, row_first = place[0] == 0, place[1] == 0

    def layer(at, lower):
        a, b = near[at], cross[at]
        return jnp.where(core_first, b, a) if lower else jnp.where(core_first, a, b)

    def row(k, c, lower):
        a, b = one[k, :, col(c)], two[k, :, col(c)]
        return jnp.where(row_first, b, a) if lower else jnp.where(row_first, a, b)

    return layer, row


def shade(light, mid, before, after, lows, highs, masks):
    lx, ly, lz = light
    first, last, head, tail = masks
    nc = len(mid[0])
    zs = [col_neighbours(mid[h], first, last) for h in range(2)]
    out = [[None] * nc, [None] * nc]
    for c in range(nc):
        ys = row_neighbours(mid[0][c], mid[1][c], lows(c), highs(c), head, tail)
        for h in range(2):
            dx = after(h, c) - before(h, c)
            dy = ys[1][h] - ys[0][h]
            dz = zs[h][1][c] - zs[h][0][c]
            inv = lax.rsqrt(4.0 + dx * dx + dy * dy + dz * dz)
            out[h][c] = dx, dy, dz, inv, (lx * dx + ly * dy + lz * dz) * inv
    return out


def opacity(d, step):
    return d * (step - d * (step**2 / 2 - d * (step**3 / 6)))


def inner_kernel(step, light, dens, weight, square, lean, totals):
    ndep, _, ncol = dens.shape
    nc = ncol // LANES
    lx, lz = light[0], light[2]
    first, last, _, _ = ids()
    totals[0] = jnp.ones_like(totals[0])
    totals[1] = jnp.zeros_like(totals[1])

    def layer(k, inside=True):
        for h in range(2):
            mid = [dens[k, half(h), col(c)] for c in range(nc)]
            if inside:
                before, after = col_neighbours(mid, first, last)
            for c in range(nc):
                at = (half(h), col(c))
                t = totals[0, half(h), col(c)]
                w = t * opacity(mid[c], step)
                totals[0, half(h), col(c)] = t - w
                w = w * mid[c]
                weight[k, half(h), col(c)] = w
                totals[1, half(h), col(c)] += w
                if inside:
                    dx = dens[k + 1, half(h), col(c)] - dens[k - 1, half(h), col(c)]
                    dz = after[c] - before[c]
                    square[k, half(h), col(c)] = 4.0 + dx * dx + dz * dz
                    lean[k, half(h), col(c)] = lx * dx + lz * dz

    layer(0, False)
    pl.loop(1, ndep - 1, unroll=3)(layer)
    layer(ndep - 1, False)


def forward_kernel(
    step, place, light, tint, dens, cot, weight, square, lean, totals, near, cross, one, two,
    packed, ends, rho, colour, rims,
):
    ndep, _, ncol = dens.shape
    nc = ncol // LANES
    lights = light[0], light[1], light[2]
    masks = ids()
    outer, beyond = facing(place, near, cross, one, two)
    rims[...] = jnp.zeros_like(rims)
    colour[...] = totals[1]

    def edges(k):
        lows, highs = [beyond(k, c, True) for c in range(nc)], [beyond(k, c, False) for c in range(nc)]
        for c in range(nc):
            rims[0, :, col(c)] += lows[c]
            rims[1, :, col(c)] += highs[c]
        return lows, highs

    def outermost(k, before, after):
        lows, highs = edges(k)
        mid = [[dens[k, half(h), col(c)] for c in range(nc)] for h in range(2)]
        tiles = shade(
            lights, mid, before, after, lambda c: wide(lows[c]), lambda c: wide(highs[c]), masks
        )
        for c in range(nc):
            for h in range(2):
                colour[half(h), col(c)] += weight[k, half(h), col(c)] * tiles[h][c][4]

    def layer(k):
        lows, highs = edges(k)
        for c in range(nc):
            top, bottom = dens[k, half(0), col(c)], dens[k, half(1), col(c)]
            before, after = row_neighbours(
                top, bottom, wide(lows[c]), wide(highs[c]), masks[2], masks[3]
            )
            for h in range(2):
                cell = (k, half(h), col(c))
                dy = after[h] - before[h]
                inv = lax.rsqrt(square[cell] + dy * dy)
                colour[half(h), col(c)] += weight[cell] * ((lean[cell] + lights[1] * dy) * inv)

    outermost(
        0, lambda h, c: outer((half(h), col(c)), True), lambda h, c: dens[1, half(h), col(c)]
    )
    outermost(
        ndep - 1,
        lambda h, c: dens[ndep - 2, half(h), col(c)],
        lambda h, c: outer((half(h), col(c)), False),
    )
    pl.loop(1, ndep - 1, unroll=5)(layer)

    passed = [1.0 - absorbed(rims[n] * step, 7) for n in range(2)]
    for c in range(nc):
        cs = slice(c * LANES, (c + 1) * LANES)
        for h in range(2):
            at = (half(h), col(c))
            t, e = totals[0, half(h), col(c)], 0.5 * colour[at]
            r = cot[0, half(h), col(c)] * tint[0]
            r = r + cot[1, half(h), col(c)] * tint[1]
            r = r + cot[2, half(h), col(c)] * tint[2]
            rho[at] = r
            ends[0, half(h), col(c)] = t
            ends[1, half(h), col(c)] = e
            v = e * r
            for b in range(4):
                a = h * 4 + b
                p = a * nc + c
                packed[p, :, 0:128] = t[2 * b : 2 * b + 1]
                packed[p, :, 128:256] = t[2 * b + 1 : 2 * b + 2]
                packed[p, :, 256:384] = passed[a // 4][:, cs]
                packed[p, :, 384:512] = v[2 * b : 2 * b + 1]
                packed[p, :, 512:640] = v[2 * b + 1 : 2 * b + 2]


def adjoint_kernel(
    step, depth, place, light, dens, near, cross, one, two, rho, ends,
    parts, adj_y, adj_z, to_near, to_cross, row_one, row_two,
    held, xs, ys, zs, trans, colour, in_sems, y_sems, z_sems,
):
    ndep, _, ncol = dens.shape
    nc = ncol // LANES
    lx, ly, lz = lights = light[0], light[1], light[2]
    masks = ids()
    core_first, row_first = place[0] == 0, place[1] == 0
    outer, beyond = facing(place, near, cross, one, two)
    blocks = ndep // BLOCK
    arrivals = []
    for b in range(blocks):
        at = pl.ds(b * BLOCK, BLOCK)
        arrivals.append(
            pltpu.make_async_copy(dens.at[at], held.at[pl.ds(b * BLOCK + 1, BLOCK)], in_sems.at[b])
        )
        arrivals[-1].start()
    for c in range(nc):
        for h in range(2):
            at = (half(h), col(c))
            held[0, half(h), col(c)] = outer(at, True)
            held[ndep + 1, half(h), col(c)] = outer(at, False)
            trans[at] = jnp.ones((8, LANES), jnp.float32)
            colour[at] = jnp.zeros((8, LANES), jnp.float32)
            for k in (0, 1):
                xs[k, half(h), col(c)] = jnp.zeros((8, LANES), jnp.float32)
            parts[0, half(h), col(c)] = jnp.zeros((8, LANES), jnp.float32)

    def layer(k):
        mid = [[held[k + 1, half(h), col(c)] for c in range(nc)] for h in range(2)]
        tiles = shade(
            lights, mid,
            lambda h, c: held[k, half(h), col(c)], lambda h, c: held[k + 2, half(h), col(c)],
            lambda c: wide(beyond(k, c, True)), lambda c: wide(beyond(k, c, False)), masks,
        )
        for c in range(nc):
            outermost = []
            for h in range(2):
                at = (half(h), col(c))
                d = mid[h][c]
                dx, dy, dz, inv, q = tiles[h][c]
                lit = 0.5 + 0.5 * q
                t = trans[at]
                w = t * opacity(d, step)
                t = t - w
                trans[at] = t
                wd = w * d
                e = colour[at] + wd * lit
                colour[at] = e
                r = rho[at] * depth
                glow = r * (w * lit + step * (t * (d * lit) + e))
                s = wd * inv * (0.5 * r)
                m = q * inv
                x = s * (lx - m * dx)
                y = s * (ly - m * dy)
                xs[k + 2, half(h), col(c)] = x
                ys[k, half(h), col(c)] = y
                zs[k, half(h), col(c)] = s * (lz - m * dz)
                parts[k + 1, half(h), col(c)] = glow
                parts[k, half(h), col(c)] += xs[k, half(h), col(c)] - x
                outermost.append(y[7 * h : 7 * h + 1])
            top, bottom = outermost
            row_one[k, :, col(c)] = jnp.where(row_first, bottom, top)
            row_two[k, :, col(c)] = jnp.where(row_first, top, bottom)

    copies = []

    def send(source, target, start, count, sem):
        at = pl.ds(start, count)
        copies.append(pltpu.make_async_copy(source.at[at], target.at[at], sem))
        copies[-1].start()

    arrivals[0].wait()
    for b in range(blocks):
        if b < blocks - 1:
            arrivals[b + 1].wait()
        pl.loop(b * BLOCK, (b + 1) * BLOCK, unroll=4)(layer)
        send(ys, adj_y, b * BLOCK, BLOCK, y_sems.at[b])
        send(zs, adj_z, b * BLOCK, BLOCK, z_sems.at[b])
    for c in range(nc):
        for h in range(2):
            at = (half(h), col(c))
            parts[ndep, half(h), col(c)] += xs[ndep, half(h), col(c)]
            first_x = xs[2, half(h), col(c)]
            last_x = xs[ndep + 1, half(h), col(c)] / ends[0, half(h), col(c)]
            to_near[at] = jnp.where(core_first, last_x, first_x)
            to_cross[at] = jnp.where(core_first, first_x, last_x)
    for copy in copies:
        copy.wait()


def scan_kernel(packed, out):
    slabs = packed.shape[0]
    front = jnp.ones((1, 384), jnp.float32)
    for m in range(slabs):
        out[m, :, 0:384] = front
        if m < slabs - 1:
            front = front * packed[m, :, 0:384]
    behind = jnp.zeros((1, 256), jnp.float32)
    for m in reversed(range(slabs)):
        out[m, :, 384:640] = behind
        if m:
            behind = behind + out[m, :, 0:256] * packed[m, :, 384:640]


def combine_kernel(
    step, depth, place, scanned, x_near, x_cross, y_one, y_two, rho, ends, parts, adj_y, adj_z,
    out, front, base, edge, ys, zs, buf, y_sems, z_sems, out_sems,
):
    ndep, _, ncol = out.shape
    nc = ncol // LANES
    first, last, head, tail = ids()
    outer, beyond = facing(place, x_near, x_cross, y_one, y_two)
    blocks = ndep // BLOCK
    arrivals = []
    for b in range(blocks):
        at = pl.ds(b * BLOCK, BLOCK)
        arrivals.append(
            [
                pltpu.make_async_copy(source.at[at], target.at[at], sems.at[b])
                for source, target, sems in ((adj_y, ys, y_sems), (adj_z, zs, z_sems))
            ]
        )
        for copy in arrivals[-1]:
            copy.start()
    for c in range(nc):
        for a in range(8):
            p = a * nc + c
            front[2 * a : 2 * a + 1, col(c)] = scanned[p, :, 0:128]
            front[2 * a + 1 : 2 * a + 2, col(c)] = scanned[p, :, 128:256]
            base[2 * a : 2 * a + 1, col(c)] = scanned[p, :, 384:512]
            base[2 * a + 1 : 2 * a + 2, col(c)] = scanned[p, :, 512:640]
        edge[0, :, col(c)] = scanned[c, :, 256:384]
        edge[1, :, col(c)] = scanned[7 * nc + c, :, 256:384]
    for c in range(nc):
        for h in range(2):
            at = (half(h), col(c))
            base[at] = (depth * step) * (base[at] + front[at] * (rho[at] * ends[1, half(h), col(c)]))

    def layer(k):
        zt, yt = [[], []], [[], []]
        for h in range(2):
            for c in range(nc):
                f = front[half(h), col(c)]
                zt[h].append(f * zs[k, half(h), col(c)])
                yt[h].append(f * ys[k, half(h), col(c)])
        zn = [col_neighbours(zt[h], first, last) for h in range(2)]
        for c in range(nc):
            lo = wide(edge[0, :, col(c)] * beyond(k, c, True))
            hi = wide(edge[1, :, col(c)] * beyond(k, c, False))
            yn = row_neighbours(yt[0][c], yt[1][c], lo, hi, head, tail)
            for h in range(2):
                at, cell = (half(h), col(c)), (k, half(h), col(c))
                own = parts[k + 1, half(h), col(c)]
                buf[cell] = (front[at] * own - base[at]) + (
                    (yn[0][h] - yn[1][h]) + (zn[h][0][c] - zn[h][1][c])
                )

    copies = []
    for b in range(blocks):
        start, stop = b * BLOCK, (b + 1) * BLOCK
        for copy in arrivals[b]:
            copy.wait()
        pl.loop(start, stop, unroll=8)(layer)
        for c in range(nc):
            for h in range(2):
                at = (half(h), col(c))
                if b == 0:
                    buf[0, half(h), col(c)] += front[at] * outer(at, True)
                if stop == ndep:
                    x = outer(at, False) * ends[0, half(h), col(c)]
                    buf[ndep - 1, half(h), col(c)] -= front[at] * x
        at = pl.ds(b * BLOCK, BLOCK)
        copies.append(pltpu.make_async_copy(buf.at[at], out.at[at], out_sems.at[b]))
        copies[-1].start()
    for copy in copies:
        copy.wait()


def params(mib):
    return pltpu.CompilerParams(vmem_limit_bytes=mib << 20)


def cost(flops, nbytes):
    return pl.CostEstimate(flops=flops, bytes_accessed=nbytes, transcendentals=0)


def near_memory(*arrays):
    return [pltpu.with_memory_space_constraint(a, pltpu.VMEM) for a in arrays]


def far_memory(*arrays):
    return [pltpu.with_memory_space_constraint(a, pltpu.HBM) for a in arrays]


def local(density, light_dir, colour_tint, cotangent):
    ndep, nrow, ncol = density.shape
    slabs = lax.axis_size(RAY)
    rows = lax.axis_size("row")
    full_depth = float(ndep * slabs)
    step = EXTINCTION / full_depth
    place = jnp.stack([lax.axis_index(RAY[2]), lax.axis_index("row") % 2]).astype(jnp.int32)

    def pairs(start, stop):
        return [(i + n, i + 1 - n) for i in range(start, stop - 1, 2) for n in range(2)]

    def exchange(row_one, row_two, to_near, to_cross):
        return near_memory(
            lax.ppermute(to_near, RAY[2], pairs(0, 2)),
            lax.ppermute(to_cross, RAY, pairs(1, slabs)),
            lax.ppermute(row_one, "row", pairs(0, rows)),
            lax.ppermute(row_two, "row", pairs(1, rows)),
        )

    def vmem(*shape):
        return pltpu.VMEM(shape, jnp.float32)

    def hbm(*shape):
        return pltpu.HBM(shape, jnp.float32)

    cube, layer, rim = (ndep, nrow, ncol), (nrow, ncol), (ndep, 1, ncol)
    share = (slabs, 1, 5 * LANES)
    blocks = ndep // BLOCK
    cells = ndep * nrow * ncol
    sem = pltpu.SemaphoreType.DMA
    held, held_cot, *pieces = pl.pallas_call(
        gather_kernel,
        out_shape=(vmem(*cube), vmem(*cotangent.shape), vmem(*rim), vmem(*rim), vmem(*layer), vmem(*layer)),
        in_specs=[SM, HBM, HBM],
        out_specs=[VM] * 6,
        scratch_shapes=[sem((ndep // PIECE,)), sem],
        compiler_params=params(4),
        name="gather",
    )(place, *far_memory(density, cotangent))
    halos = exchange(*pieces)
    inner = pl.pallas_call(
        functools.partial(inner_kernel, step),
        out_shape=(vmem(*cube),) * 3 + (vmem(2, *layer),),
        in_specs=[SM, VM],
        out_specs=[VM] * 4,
        compiler_params=params(4),
        cost_estimate=cost(50 * cells, 16 * cells),
        name="inner",
    )(light_dir, held)
    packed, ends, rho = pl.pallas_call(
        functools.partial(forward_kernel, step),
        out_shape=(vmem(*share), vmem(2, *layer), vmem(*layer)),
        in_specs=[SM, SM, SM] + [VM] * 10,
        out_specs=[VM] * 3,
        scratch_shapes=[vmem(*layer), vmem(2, 1, ncol)],
        compiler_params=params(4),
        cost_estimate=cost(30 * cells, 4 * cells),
        name="forward",
    )(place, light_dir, colour_tint, held, held_cot, *inner, *halos)

    scanned = lax.all_to_all(packed, RAY, 0, 0)
    part, adj_y, adj_z, to_near, to_cross, row_one, row_two = pl.pallas_call(
        functools.partial(adjoint_kernel, step, full_depth),
        out_shape=(vmem(ndep + 1, nrow, ncol), hbm(*cube), hbm(*cube))
        + (vmem(*layer), vmem(*layer), vmem(*rim), vmem(*rim)),
        in_specs=[SM, SM, HBM] + [VM] * 6,
        out_specs=[VM, HBM, HBM] + [VM] * 4,
        scratch_shapes=[
            vmem(ndep + 2, nrow, ncol),
            vmem(ndep + 2, nrow, ncol),
            vmem(*cube),
            vmem(*cube),
            vmem(*layer),
            vmem(*layer),
            sem((blocks,)),
            sem((blocks,)),
            sem((blocks,)),
        ],
        compiler_params=params(16),
        cost_estimate=cost(70 * cells, 16 * cells),
        name="adjoint",
    )(place, light_dir, *far_memory(density), *halos, rho, ends)
    scanned, to_near, to_cross, row_one, row_two = lax.optimization_barrier(
        (scanned, to_near, to_cross, row_one, row_two)
    )
    scanned = pl.pallas_call(
        scan_kernel,
        out_shape=vmem(*share),
        in_specs=[VM],
        out_specs=VM,
        compiler_params=params(4),
        name="scan",
    )(*near_memory(scanned))
    scanned = lax.all_to_all(scanned, RAY, 0, 0)
    rims = exchange(row_one, row_two, to_near, to_cross)
    return pl.pallas_call(
        functools.partial(combine_kernel, step, full_depth),
        out_shape=sds(*cube),
        in_specs=[SM] + [VM] * 8 + [HBM] * 2,
        out_specs=HBM,
        scratch_shapes=[
            vmem(*layer),
            vmem(*layer),
            vmem(2, 1, ncol),
            vmem(*cube),
            vmem(*cube),
            vmem(*cube),
            sem((blocks,)),
            sem((blocks,)),
            sem((blocks,)),
        ],
        compiler_params=params(16),
        cost_estimate=cost(12 * cells, 16 * cells),
        name="combine",
    )(place, *near_memory(scanned), *rims, rho, ends, part, *far_memory(adj_y, adj_z))


def solution(mesh):
    torus = Mesh(
        mesh.devices.reshape(4, 8, 2, mesh.shape["row"]), ("ray_0", "ray_1", "ray_2", "row")
    )
    placed = (P(RAY, "row", None), P(), P(), P(None, "row", None))
    return jax.shard_map(
        local, mesh=torus, in_specs=placed, out_specs=P(RAY, "row", None), check_vma=False
    )
```

```python
import functools

import jax
import jax.numpy as jnp
from jax import lax
from jax.experimental import pallas as pl
from jax.experimental.pallas import tpu as pltpu
from jax.sharding import Mesh
from jax.sharding import PartitionSpec as P

RAY = ("ray_0", "ray_1", "ray_2")
EXTINCTION = 0.7
LANES = 128
BLOCK = 8
PIECE = 4
CUTS = (0, 4, 12, 20, 28, 32)
VM = pl.BlockSpec(memory_space=pltpu.VMEM)
SM = pl.BlockSpec(memory_space=pltpu.SMEM)
HBM = pl.BlockSpec(memory_space=pltpu.HBM)


def sds(*shape):
    return jax.ShapeDtypeStruct(shape, jnp.float32)


def col(c):
    return pl.ds(c * LANES, LANES)


def half(h):
    return pl.ds(h * 8, 8)


def ids():
    lane = lax.broadcasted_iota(jnp.int32, (8, LANES), 1)
    sub = lax.broadcasted_iota(jnp.int32, (8, LANES), 0)
    return lane == 0, lane == LANES - 1, sub == 0, sub == 7


def wide(row):
    return jnp.broadcast_to(row, (8, LANES))


def col_neighbours(tiles, first, last):
    right = [pltpu.roll(t, 1, 1) for t in tiles]
    left = [pltpu.roll(t, LANES - 1, 1) for t in tiles]
    zero = jnp.zeros((8, LANES), jnp.float32)
    n = len(tiles)
    before = [jnp.where(first, right[c - 1] if c else zero, right[c]) for c in range(n)]
    after = [jnp.where(last, left[c + 1] if c < n - 1 else zero, left[c]) for c in range(n)]
    return before, after


def row_neighbours(top, bottom, above, below, first, last):
    down = [pltpu.roll(t, 1, 0) for t in (top, bottom)]
    up = [pltpu.roll(t, 7, 0) for t in (top, bottom)]
    before = (jnp.where(first, above, down[0]), jnp.where(first, down[0], down[1]))
    after = (jnp.where(last, up[1], up[0]), jnp.where(last, below, up[1]))
    return before, after


def absorbed(optical, terms):
    value = 1.0 - optical * (1.0 / terms)
    for n in range(terms - 1, 1, -1):
        value = 1.0 - optical * (1.0 / n) * value
    return optical * value


def gather_kernel(place, dens, cot, held, held_cot, row_one, row_two, to_near, to_cross, sems, cot_sem):
    ndep, nrow, _ = dens.shape
    core_first, row_first = place[0] == 0, place[1] == 0
    colours = pltpu.make_async_copy(cot, held_cot, cot_sem)
    copies = []
    for b in range(ndep // PIECE):
        part = pl.ds(b * PIECE, PIECE)
        copies.append(pltpu.make_async_copy(dens.at[part], held.at[part], sems.at[b]))
        copies[-1].start()
    colours.start()
    for b, copy in enumerate(copies):
        copy.wait()
        for k in range(b * PIECE, (b + 1) * PIECE):
            top, bottom = held[k, 0:1, :], held[k, nrow - 1 : nrow, :]
            row_one[k] = jnp.where(row_first, bottom, top)
            row_two[k] = jnp.where(row_first, top, bottom)
    first_layer, last_layer = held[0], held[ndep - 1]
    to_near[...] = jnp.where(core_first, last_layer, first_layer)
    to_cross[...] = jnp.where(core_first, first_layer, last_layer)
    colours.wait()


def facing(place, near, cross, one, two):
    core_first, row_first = place[0] == 0, place[1] == 0

    def layer(at, lower):
        a, b = near[at], cross[at]
        return jnp.where(core_first, b, a) if lower else jnp.where(core_first, a, b)

    def row(k, c, lower):
        a, b = one[k, :, col(c)], two[k, :, col(c)]
        return jnp.where(row_first, b, a) if lower else jnp.where(row_first, a, b)

    return layer, row


def shade(light, mid, before, after, lows, highs, masks):
    lx, ly, lz = light
    first, last, head, tail = masks
    nc = len(mid[0])
    zs = [col_neighbours(mid[h], first, last) for h in range(2)]
    out = [[None] * nc, [None] * nc]
    for c in range(nc):
        ys = row_neighbours(mid[0][c], mid[1][c], lows(c), highs(c), head, tail)
        for h in range(2):
            dx = after(h, c) - before(h, c)
            dy = ys[1][h] - ys[0][h]
            dz = zs[h][1][c] - zs[h][0][c]
            inv = lax.rsqrt(4.0 + dx * dx + dy * dy + dz * dz)
            out[h][c] = dx, dy, dz, inv, (lx * dx + ly * dy + lz * dz) * inv
    return out


def opacity(d, step):
    return d * (step - d * (step**2 / 2 - d * (step**3 / 6)))


def inner_kernel(step, light, dens, weight, square, lean, totals):
    ndep, _, ncol = dens.shape
    nc = ncol // LANES
    lx, lz = light[0], light[2]
    first, last, _, _ = ids()
    totals[0] = jnp.ones_like(totals[0])
    totals[1] = jnp.zeros_like(totals[1])

    def layer(k, inside=True):
        for h in range(2):
            mid = [dens[k, half(h), col(c)] for c in range(nc)]
            if inside:
                before, after = col_neighbours(mid, first, last)
            for c in range(nc):
                at = (half(h), col(c))
                t = totals[0, half(h), col(c)]
                w = t * opacity(mid[c], step)
                totals[0, half(h), col(c)] = t - w
                w = w * mid[c]
                weight[k, half(h), col(c)] = w
                totals[1, half(h), col(c)] += w
                if inside:
                    dx = dens[k + 1, half(h), col(c)] - dens[k - 1, half(h), col(c)]
                    dz = after[c] - before[c]
                    square[k, half(h), col(c)] = 4.0 + dx * dx + dz * dz
                    lean[k, half(h), col(c)] = lx * dx + lz * dz

    layer(0, False)
    pl.loop(1, ndep - 1, unroll=6)(layer)
    layer(ndep - 1, False)


def forward_kernel(
    step, place, light, tint, dens, cot, weight, square, lean, totals, near, cross, one, two,
    packed, ends, rho, colour, rims,
):
    ndep, _, ncol = dens.shape
    nc = ncol // LANES
    lights = light[0], light[1], light[2]
    masks = ids()
    outer, beyond = facing(place, near, cross, one, two)
    rims[...] = jnp.zeros_like(rims)
    colour[...] = totals[1]

    def edges(k):
        lows, highs = [beyond(k, c, True) for c in range(nc)], [beyond(k, c, False) for c in range(nc)]
        for c in range(nc):
            rims[0, :, col(c)] += lows[c]
            rims[1, :, col(c)] += highs[c]
        return lows, highs

    def outermost(k, before, after):
        lows, highs = edges(k)
        mid = [[dens[k, half(h), col(c)] for c in range(nc)] for h in range(2)]
        tiles = shade(
            lights, mid, before, after, lambda c: wide(lows[c]), lambda c: wide(highs[c]), masks
        )
        for c in range(nc):
            for h in range(2):
                colour[half(h), col(c)] += weight[k, half(h), col(c)] * tiles[h][c][4]

    def layer(k):
        lows, highs = edges(k)
        for c in range(nc):
            top, bottom = dens[k, half(0), col(c)], dens[k, half(1), col(c)]
            before, after = row_neighbours(
                top, bottom, wide(lows[c]), wide(highs[c]), masks[2], masks[3]
            )
            for h in range(2):
                cell = (k, half(h), col(c))
                dy = after[h] - before[h]
                inv = lax.rsqrt(square[cell] + dy * dy)
                colour[half(h), col(c)] += weight[cell] * ((lean[cell] + lights[1] * dy) * inv)

    outermost(
        0, lambda h, c: outer((half(h), col(c)), True), lambda h, c: dens[1, half(h), col(c)]
    )
    outermost(
        ndep - 1,
        lambda h, c: dens[ndep - 2, half(h), col(c)],
        lambda h, c: outer((half(h), col(c)), False),
    )
    pl.loop(1, ndep - 1, unroll=10)(layer)

    passed = [1.0 - absorbed(rims[n] * step, 7) for n in range(2)]
    for c in range(nc):
        cs = slice(c * LANES, (c + 1) * LANES)
        for h in range(2):
            at = (half(h), col(c))
            t, e = totals[0, half(h), col(c)], 0.5 * colour[at]
            r = cot[0, half(h), col(c)] * tint[0]
            r = r + cot[1, half(h), col(c)] * tint[1]
            r = r + cot[2, half(h), col(c)] * tint[2]
            rho[at] = r
            ends[0, half(h), col(c)] = t
            ends[1, half(h), col(c)] = e
            v = e * r
            for b in range(4):
                a = h * 4 + b
                p = a * nc + c
                packed[p, :, 0:128] = t[2 * b : 2 * b + 1]
                packed[p, :, 128:256] = t[2 * b + 1 : 2 * b + 2]
                packed[p, :, 256:384] = passed[a // 4][:, cs]
                packed[p, :, 384:512] = v[2 * b : 2 * b + 1]
                packed[p, :, 512:640] = v[2 * b + 1 : 2 * b + 2]


def adjoint_kernel(
    step, depth, place, light, dens, near, cross, one, two, rho, ends,
    parts, adj_y, adj_z, to_near, to_cross, row_one, row_two,
    held, xs, ys, zs, trans, colour, in_sems, y_sems, z_sems,
):
    ndep, _, ncol = dens.shape
    nc = ncol // LANES
    lx, ly, lz = lights = light[0], light[1], light[2]
    masks = ids()
    core_first, row_first = place[0] == 0, place[1] == 0
    outer, beyond = facing(place, near, cross, one, two)
    blocks = ndep // BLOCK
    arrivals = []
    for b in range(blocks):
        at = pl.ds(b * BLOCK, BLOCK)
        arrivals.append(
            pltpu.make_async_copy(dens.at[at], held.at[pl.ds(b * BLOCK + 1, BLOCK)], in_sems.at[b])
        )
        arrivals[-1].start()
    for c in range(nc):
        for h in range(2):
            at = (half(h), col(c))
            held[0, half(h), col(c)] = outer(at, True)
            held[ndep + 1, half(h), col(c)] = outer(at, False)
            trans[at] = jnp.ones((8, LANES), jnp.float32)
            colour[at] = jnp.zeros((8, LANES), jnp.float32)
            for k in (0, 1):
                xs[k, half(h), col(c)] = jnp.zeros((8, LANES), jnp.float32)
            parts[0, half(h), col(c)] = jnp.zeros((8, LANES), jnp.float32)

    def layer(k):
        mid = [[held[k + 1, half(h), col(c)] for c in range(nc)] for h in range(2)]
        tiles = shade(
            lights, mid,
            lambda h, c: held[k, half(h), col(c)], lambda h, c: held[k + 2, half(h), col(c)],
            lambda c: wide(beyond(k, c, True)), lambda c: wide(beyond(k, c, False)), masks,
        )
        for c in range(nc):
            outermost = []
            for h in range(2):
                at = (half(h), col(c))
                d = mid[h][c]
                dx, dy, dz, inv, q = tiles[h][c]
                lit = 0.5 + 0.5 * q
                t = trans[at]
                w = t * opacity(d, step)
                t = t - w
                trans[at] = t
                wd = w * d
                e = colour[at] + wd * lit
                colour[at] = e
                r = rho[at] * depth
                glow = r * (w * lit + step * (t * (d * lit) + e))
                s = wd * inv * (0.5 * r)
                m = q * inv
                x = s * (lx - m * dx)
                y = s * (ly - m * dy)
                xs[k + 2, half(h), col(c)] = x
                ys[k, half(h), col(c)] = y
                zs[k, half(h), col(c)] = s * (lz - m * dz)
                parts[k + 1, half(h), col(c)] = glow
                parts[k, half(h), col(c)] += xs[k, half(h), col(c)] - x
                outermost.append(y[7 * h : 7 * h + 1])
            top, bottom = outermost
            row_one[k, :, col(c)] = jnp.where(row_first, bottom, top)
            row_two[k, :, col(c)] = jnp.where(row_first, top, bottom)

    copies = []

    def send(source, target, start, count, sem):
        at = pl.ds(start, count)
        copies.append(pltpu.make_async_copy(source.at[at], target.at[at], sem))
        copies[-1].start()

    arrivals[0].wait()
    for b in range(blocks):
        if b < blocks - 1:
            arrivals[b + 1].wait()
        pl.loop(b * BLOCK, (b + 1) * BLOCK, unroll=4)(layer)
        send(ys, adj_y, b * BLOCK, BLOCK, y_sems.at[b])
        send(zs, adj_z, b * BLOCK, BLOCK, z_sems.at[b])
    for c in range(nc):
        for h in range(2):
            at = (half(h), col(c))
            parts[ndep, half(h), col(c)] += xs[ndep, half(h), col(c)]
            first_x = xs[2, half(h), col(c)]
            last_x = xs[ndep + 1, half(h), col(c)] / ends[0, half(h), col(c)]
            to_near[at] = jnp.where(core_first, last_x, first_x)
            to_cross[at] = jnp.where(core_first, first_x, last_x)
    for copy in copies:
        copy.wait()


def scan_kernel(packed, out):
    slabs = packed.shape[0]
    front = jnp.ones((1, 384), jnp.float32)
    weighed = []
    for m in range(slabs):
        out[m, :, 0:384] = front
        weighed.append(front[:, :256] * packed[m, :, 384:640])
        front = front * packed[m, :, 0:384]
    behind = jnp.zeros((1, 256), jnp.float32)
    for m in reversed(range(slabs)):
        out[m, :, 384:640] = behind
        behind = behind + weighed[m]


def combine_kernel(
    step, depth, place, scanned, x_near, x_cross, y_one, y_two, rho, ends, parts, adj_y, adj_z,
    out, front, base, edge, ys, zs, buf, y_sems, z_sems, out_sems,
):
    ndep, _, ncol = out.shape
    nc = ncol // LANES
    first, last, head, tail = ids()
    outer, beyond = facing(place, x_near, x_cross, y_one, y_two)
    spans = list(zip(CUTS[:-1], CUTS[1:]))
    arrivals = []
    for b, (start, stop) in enumerate(spans):
        at = pl.ds(start, stop - start)
        arrivals.append(
            [
                pltpu.make_async_copy(source.at[at], target.at[at], sems.at[b])
                for source, target, sems in ((adj_y, ys, y_sems), (adj_z, zs, z_sems))
            ]
        )
        for copy in arrivals[-1]:
            copy.start()
    for c in range(nc):
        for a in range(8):
            p = a * nc + c
            front[2 * a : 2 * a + 1, col(c)] = scanned[p, :, 0:128]
            front[2 * a + 1 : 2 * a + 2, col(c)] = scanned[p, :, 128:256]
            base[2 * a : 2 * a + 1, col(c)] = scanned[p, :, 384:512]
            base[2 * a + 1 : 2 * a + 2, col(c)] = scanned[p, :, 512:640]
        edge[0, :, col(c)] = scanned[c, :, 256:384]
        edge[1, :, col(c)] = scanned[7 * nc + c, :, 256:384]
    for c in range(nc):
        for h in range(2):
            at = (half(h), col(c))
            base[at] = (depth * step) * (base[at] + front[at] * (rho[at] * ends[1, half(h), col(c)]))

    def layer(k):
        zt, yt = [[], []], [[], []]
        for h in range(2):
            for c in range(nc):
                f = front[half(h), col(c)]
                zt[h].append(f * zs[k, half(h), col(c)])
                yt[h].append(f * ys[k, half(h), col(c)])
        zn = [col_neighbours(zt[h], first, last) for h in range(2)]
        for c in range(nc):
            lo = wide(edge[0, :, col(c)] * beyond(k, c, True))
            hi = wide(edge[1, :, col(c)] * beyond(k, c, False))
            yn = row_neighbours(yt[0][c], yt[1][c], lo, hi, head, tail)
            for h in range(2):
                at, cell = (half(h), col(c)), (k, half(h), col(c))
                own = parts[k + 1, half(h), col(c)]
                buf[cell] = (front[at] * own - base[at]) + (
                    (yn[0][h] - yn[1][h]) + (zn[h][0][c] - zn[h][1][c])
                )

    copies = []
    for b, (start, stop) in enumerate(spans):
        for copy in arrivals[b]:
            copy.wait()
        pl.loop(start, stop, unroll=stop - start)(layer)
        for c in range(nc):
            for h in range(2):
                at = (half(h), col(c))
                if b == 0:
                    buf[0, half(h), col(c)] += front[at] * outer(at, True)
                if stop == ndep:
                    x = outer(at, False) * ends[0, half(h), col(c)]
                    buf[ndep - 1, half(h), col(c)] -= front[at] * x
        at = pl.ds(start, stop - start)
        copies.append(pltpu.make_async_copy(buf.at[at], out.at[at], out_sems.at[b]))
        copies[-1].start()
    for copy in copies:
        copy.wait()


def params(mib):
    return pltpu.CompilerParams(vmem_limit_bytes=mib << 20)


def cost(flops, nbytes):
    return pl.CostEstimate(flops=flops, bytes_accessed=nbytes, transcendentals=0)


def near_memory(*arrays):
    return [pltpu.with_memory_space_constraint(a, pltpu.VMEM) for a in arrays]


def far_memory(*arrays):
    return [pltpu.with_memory_space_constraint(a, pltpu.HBM) for a in arrays]


def local(density, light_dir, colour_tint, cotangent):
    ndep, nrow, ncol = density.shape
    slabs = lax.axis_size(RAY)
    rows = lax.axis_size("row")
    full_depth = float(ndep * slabs)
    step = EXTINCTION / full_depth
    place = jnp.stack([lax.axis_index(RAY[2]), lax.axis_index("row") % 2]).astype(jnp.int32)

    def pairs(start, stop):
        return [(i + n, i + 1 - n) for i in range(start, stop - 1, 2) for n in range(2)]

    def exchange(row_one, row_two, to_near, to_cross):
        return near_memory(
            lax.ppermute(to_near, RAY[2], pairs(0, 2)),
            lax.ppermute(to_cross, RAY, pairs(1, slabs)),
            lax.ppermute(row_one, "row", pairs(0, rows)),
            lax.ppermute(row_two, "row", pairs(1, rows)),
        )

    def vmem(*shape):
        return pltpu.VMEM(shape, jnp.float32)

    def hbm(*shape):
        return pltpu.HBM(shape, jnp.float32)

    cube, layer, rim = (ndep, nrow, ncol), (nrow, ncol), (ndep, 1, ncol)
    share = (slabs, 1, 5 * LANES)
    blocks = ndep // BLOCK
    cells = ndep * nrow * ncol
    sem = pltpu.SemaphoreType.DMA
    held, held_cot, *pieces = pl.pallas_call(
        gather_kernel,
        out_shape=(vmem(*cube), vmem(*cotangent.shape), vmem(*rim), vmem(*rim), vmem(*layer), vmem(*layer)),
        in_specs=[SM, HBM, HBM],
        out_specs=[VM] * 6,
        scratch_shapes=[sem((ndep // PIECE,)), sem],
        compiler_params=params(4),
        name="gather",
    )(place, *far_memory(density, cotangent))
    halos = exchange(*pieces)
    inner = pl.pallas_call(
        functools.partial(inner_kernel, step),
        out_shape=(vmem(*cube),) * 3 + (vmem(2, *layer),),
        in_specs=[SM, VM],
        out_specs=[VM] * 4,
        compiler_params=params(4),
        cost_estimate=cost(50 * cells, 16 * cells),
        name="inner",
    )(light_dir, held)
    packed, ends, rho = pl.pallas_call(
        functools.partial(forward_kernel, step),
        out_shape=(vmem(*share), vmem(2, *layer), vmem(*layer)),
        in_specs=[SM, SM, SM] + [VM] * 10,
        out_specs=[VM] * 3,
        scratch_shapes=[vmem(*layer), vmem(2, 1, ncol)],
        compiler_params=params(4),
        cost_estimate=cost(30 * cells, 4 * cells),
        name="forward",
    )(place, light_dir, colour_tint, held, held_cot, *inner, *halos)

    scanned = lax.all_to_all(packed, RAY, 0, 0)
    part, adj_y, adj_z, to_near, to_cross, row_one, row_two = pl.pallas_call(
        functools.partial(adjoint_kernel, step, full_depth),
        out_shape=(vmem(ndep + 1, nrow, ncol), hbm(*cube), hbm(*cube))
        + (vmem(*layer), vmem(*layer), vmem(*rim), vmem(*rim)),
        in_specs=[SM, SM, HBM] + [VM] * 6,
        out_specs=[VM, HBM, HBM] + [VM] * 4,
        scratch_shapes=[
            vmem(ndep + 2, nrow, ncol),
            vmem(ndep + 2, nrow, ncol),
            vmem(*cube),
            vmem(*cube),
            vmem(*layer),
            vmem(*layer),
            sem((blocks,)),
            sem((blocks,)),
            sem((blocks,)),
        ],
        compiler_params=params(16),
        cost_estimate=cost(70 * cells, 16 * cells),
        name="adjoint",
    )(place, light_dir, *far_memory(density), *halos, rho, ends)
    scanned, to_near, to_cross, row_one, row_two = lax.optimization_barrier(
        (scanned, to_near, to_cross, row_one, row_two)
    )
    scanned = pl.pallas_call(
        scan_kernel,
        out_shape=vmem(*share),
        in_specs=[VM],
        out_specs=VM,
        compiler_params=params(4),
        name="scan",
    )(*near_memory(scanned))
    scanned = lax.all_to_all(scanned, RAY, 0, 0)
    rims = exchange(row_one, row_two, to_near, to_cross)
    return pl.pallas_call(
        functools.partial(combine_kernel, step, full_depth),
        out_shape=sds(*cube),
        in_specs=[SM] + [VM] * 8 + [HBM] * 2,
        out_specs=HBM,
        scratch_shapes=[
            vmem(*layer),
            vmem(*layer),
            vmem(2, 1, ncol),
            vmem(*cube),
            vmem(*cube),
            vmem(*cube),
            sem((len(CUTS),)),
            sem((len(CUTS),)),
            sem((len(CUTS),)),
        ],
        compiler_params=params(16),
        cost_estimate=cost(12 * cells, 16 * cells),
        name="combine",
    )(place, *near_memory(scanned), *rims, rho, ends, part, *far_memory(adj_y, adj_z))


def solution(mesh):
    torus = Mesh(
        mesh.devices.reshape(4, 8, 2, mesh.shape["row"]), ("ray_0", "ray_1", "ray_2", "row")
    )
    placed = (P(RAY, "row", None), P(), P(), P(None, "row", None))
    return jax.shard_map(
        local, mesh=torus, in_specs=placed, out_specs=P(RAY, "row", None), check_vma=False
    )
```

```python
import functools

import jax
import jax.numpy as jnp
from jax import lax
from jax.experimental import pallas as pl
from jax.experimental.pallas import tpu as pltpu
from jax.sharding import Mesh
from jax.sharding import PartitionSpec as P

RAY = ("ray_0", "ray_1", "ray_2")
EXTINCTION = 0.7
LANES = 128
BLOCK = 8
PIECE = 4
CUTS = (0, 4, 12, 20, 28, 32)
VM = pl.BlockSpec(memory_space=pltpu.VMEM)
SM = pl.BlockSpec(memory_space=pltpu.SMEM)
HBM = pl.BlockSpec(memory_space=pltpu.HBM)


def sds(*shape):
    return jax.ShapeDtypeStruct(shape, jnp.float32)


def col(c):
    return pl.ds(c * LANES, LANES)


def half(h):
    return pl.ds(h * 8, 8)


def ids():
    lane = lax.broadcasted_iota(jnp.int32, (8, LANES), 1)
    sub = lax.broadcasted_iota(jnp.int32, (8, LANES), 0)
    return lane == 0, lane == LANES - 1, sub == 0, sub == 7


def wide(row):
    return jnp.broadcast_to(row, (8, LANES))


def col_neighbours(tiles, first, last):
    right = [pltpu.roll(t, 1, 1) for t in tiles]
    left = [pltpu.roll(t, LANES - 1, 1) for t in tiles]
    zero = jnp.zeros((8, LANES), jnp.float32)
    n = len(tiles)
    before = [jnp.where(first, right[c - 1] if c else zero, right[c]) for c in range(n)]
    after = [jnp.where(last, left[c + 1] if c < n - 1 else zero, left[c]) for c in range(n)]
    return before, after


def row_neighbours(top, bottom, above, below, first, last):
    down = [pltpu.roll(t, 1, 0) for t in (top, bottom)]
    up = [pltpu.roll(t, 7, 0) for t in (top, bottom)]
    before = (jnp.where(first, above, down[0]), jnp.where(first, down[0], down[1]))
    after = (jnp.where(last, up[1], up[0]), jnp.where(last, below, up[1]))
    return before, after


def absorbed(optical, terms):
    value = 1.0 - optical * (1.0 / terms)
    for n in range(terms - 1, 1, -1):
        value = 1.0 - optical * (1.0 / n) * value
    return optical * value


def gather_kernel(place, dens, cot, held, held_cot, row_one, row_two, to_near, to_cross, sems, cot_sem):
    ndep, nrow, _ = dens.shape
    core_first, row_first = place[0] == 0, place[1] == 0
    colours = pltpu.make_async_copy(cot, held_cot, cot_sem)
    copies = []
    for b in range(ndep // PIECE):
        part = pl.ds(b * PIECE, PIECE)
        copies.append(pltpu.make_async_copy(dens.at[part], held.at[part], sems.at[b]))
        copies[-1].start()
    colours.start()
    sums = [jnp.zeros((1, dens.shape[2]), jnp.float32)] * 2
    for b, copy in enumerate(copies):
        copy.wait()
        for k in range(b * PIECE, (b + 1) * PIECE):
            top, bottom = held[k, 0:1, :], held[k, nrow - 1 : nrow, :]
            row_one[k] = jnp.where(row_first, bottom, top)
            row_two[k] = jnp.where(row_first, top, bottom)
            sums = [sums[0] + top, sums[1] + bottom]
    row_one[ndep] = jnp.where(row_first, sums[1], sums[0])
    row_two[ndep] = jnp.where(row_first, sums[0], sums[1])
    first_layer, last_layer = held[0], held[ndep - 1]
    to_near[...] = jnp.where(core_first, last_layer, first_layer)
    to_cross[...] = jnp.where(core_first, first_layer, last_layer)
    colours.wait()


def facing(place, near, cross, one, two):
    core_first, row_first = place[0] == 0, place[1] == 0

    def layer(at, lower):
        a, b = near[at], cross[at]
        return jnp.where(core_first, b, a) if lower else jnp.where(core_first, a, b)

    def row(k, c, lower):
        a, b = one[k, :, col(c)], two[k, :, col(c)]
        return jnp.where(row_first, b, a) if lower else jnp.where(row_first, a, b)

    return layer, row


def shade(light, mid, before, after, lows, highs, masks):
    lx, ly, lz = light
    first, last, head, tail = masks
    nc = len(mid[0])
    zs = [col_neighbours(mid[h], first, last) for h in range(2)]
    out = [[None] * nc, [None] * nc]
    for c in range(nc):
        ys = row_neighbours(mid[0][c], mid[1][c], lows(c), highs(c), head, tail)
        for h in range(2):
            dx = after(h, c) - before(h, c)
            dy = ys[1][h] - ys[0][h]
            dz = zs[h][1][c] - zs[h][0][c]
            inv = lax.rsqrt(4.0 + dx * dx + dy * dy + dz * dz)
            out[h][c] = dx, dy, dz, inv, (lx * dx + ly * dy + lz * dz) * inv
    return out


def opacity(d, step):
    return d * (step - d * (step**2 / 2 - d * (step**3 / 6)))


def inner_kernel(step, light, dens, weight, square, lean, totals):
    ndep, _, ncol = dens.shape
    nc = ncol // LANES
    lx, lz = light[0], light[2]
    first, last, _, _ = ids()
    totals[0] = jnp.ones_like(totals[0])
    totals[1] = jnp.zeros_like(totals[1])

    def layer(k, inside=True):
        for h in range(2):
            mid = [dens[k, half(h), col(c)] for c in range(nc)]
            if inside:
                before, after = col_neighbours(mid, first, last)
            for c in range(nc):
                at = (half(h), col(c))
                t = totals[0, half(h), col(c)]
                w = t * opacity(mid[c], step)
                totals[0, half(h), col(c)] = t - w
                w = w * mid[c]
                weight[k, half(h), col(c)] = w
                totals[1, half(h), col(c)] += w
                if inside:
                    dx = dens[k + 1, half(h), col(c)] - dens[k - 1, half(h), col(c)]
                    dz = after[c] - before[c]
                    square[k, half(h), col(c)] = 4.0 + dx * dx + dz * dz
                    lean[k, half(h), col(c)] = lx * dx + lz * dz

    layer(0, False)
    pl.loop(1, ndep - 1, unroll=6)(layer)
    layer(ndep - 1, False)


def forward_kernel(
    step, place, light, tint, dens, cot, weight, square, lean, totals, near, cross, one, two,
    packed, ends, rho, colour,
):
    ndep, _, ncol = dens.shape
    nc = ncol // LANES
    lights = light[0], light[1], light[2]
    masks = ids()
    outer, beyond = facing(place, near, cross, one, two)
    colour[...] = totals[1]

    def edges(k):
        lows, highs = [beyond(k, c, True) for c in range(nc)], [beyond(k, c, False) for c in range(nc)]
        return lows, highs

    def outermost(k, before, after):
        lows, highs = edges(k)
        mid = [[dens[k, half(h), col(c)] for c in range(nc)] for h in range(2)]
        tiles = shade(
            lights, mid, before, after, lambda c: wide(lows[c]), lambda c: wide(highs[c]), masks
        )
        for c in range(nc):
            for h in range(2):
                colour[half(h), col(c)] += weight[k, half(h), col(c)] * tiles[h][c][4]

    def layer(k):
        lows, highs = edges(k)
        for c in range(nc):
            top, bottom = dens[k, half(0), col(c)], dens[k, half(1), col(c)]
            before, after = row_neighbours(
                top, bottom, wide(lows[c]), wide(highs[c]), masks[2], masks[3]
            )
            for h in range(2):
                cell = (k, half(h), col(c))
                dy = after[h] - before[h]
                inv = lax.rsqrt(square[cell] + dy * dy)
                colour[half(h), col(c)] += weight[cell] * ((lean[cell] + lights[1] * dy) * inv)

    outermost(
        0, lambda h, c: outer((half(h), col(c)), True), lambda h, c: dens[1, half(h), col(c)]
    )
    outermost(
        ndep - 1,
        lambda h, c: dens[ndep - 2, half(h), col(c)],
        lambda h, c: outer((half(h), col(c)), False),
    )
    pl.loop(1, ndep - 1, unroll=10)(layer)

    row_first = place[1] == 0
    sums = jnp.where(row_first, two[ndep], one[ndep]), jnp.where(row_first, one[ndep], two[ndep])
    passed = [1.0 - absorbed(total * step, 7) for total in sums]
    for c in range(nc):
        cs = slice(c * LANES, (c + 1) * LANES)
        for h in range(2):
            at = (half(h), col(c))
            t, e = totals[0, half(h), col(c)], 0.5 * colour[at]
            r = cot[0, half(h), col(c)] * tint[0]
            r = r + cot[1, half(h), col(c)] * tint[1]
            r = r + cot[2, half(h), col(c)] * tint[2]
            rho[at] = r
            ends[0, half(h), col(c)] = t
            ends[1, half(h), col(c)] = e
            v = e * r
            for b in range(4):
                a = h * 4 + b
                p = a * nc + c
                packed[p, :, 0:128] = t[2 * b : 2 * b + 1]
                packed[p, :, 128:256] = t[2 * b + 1 : 2 * b + 2]
                packed[p, :, 256:384] = passed[a // 4][:, cs]
                packed[p, :, 384:512] = v[2 * b : 2 * b + 1]
                packed[p, :, 512:640] = v[2 * b + 1 : 2 * b + 2]


def adjoint_kernel(
    step, depth, place, light, dens, near, cross, one, two, rho, ends,
    parts, adj_y, adj_z, to_near, to_cross, row_one, row_two,
    held, xs, ys, zs, trans, colour, in_sems, y_sems, z_sems,
):
    ndep, _, ncol = dens.shape
    nc = ncol // LANES
    lx, ly, lz = lights = light[0], light[1], light[2]
    masks = ids()
    core_first, row_first = place[0] == 0, place[1] == 0
    outer, beyond = facing(place, near, cross, one, two)
    blocks = ndep // BLOCK
    arrivals = []
    for b in range(blocks):
        at = pl.ds(b * BLOCK, BLOCK)
        arrivals.append(
            pltpu.make_async_copy(dens.at[at], held.at[pl.ds(b * BLOCK + 1, BLOCK)], in_sems.at[b])
        )
        arrivals[-1].start()
    for c in range(nc):
        for h in range(2):
            at = (half(h), col(c))
            held[0, half(h), col(c)] = outer(at, True)
            held[ndep + 1, half(h), col(c)] = outer(at, False)
            trans[at] = jnp.ones((8, LANES), jnp.float32)
            colour[at] = jnp.zeros((8, LANES), jnp.float32)
            for k in (0, 1):
                xs[k, half(h), col(c)] = jnp.zeros((8, LANES), jnp.float32)
            parts[0, half(h), col(c)] = jnp.zeros((8, LANES), jnp.float32)

    def layer(k):
        mid = [[held[k + 1, half(h), col(c)] for c in range(nc)] for h in range(2)]
        tiles = shade(
            lights, mid,
            lambda h, c: held[k, half(h), col(c)], lambda h, c: held[k + 2, half(h), col(c)],
            lambda c: wide(beyond(k, c, True)), lambda c: wide(beyond(k, c, False)), masks,
        )
        for c in range(nc):
            outermost = []
            for h in range(2):
                at = (half(h), col(c))
                d = mid[h][c]
                dx, dy, dz, inv, q = tiles[h][c]
                lit = 0.5 + 0.5 * q
                t = trans[at]
                w = t * opacity(d, step)
                t = t - w
                trans[at] = t
                wd = w * d
                e = colour[at] + wd * lit
                colour[at] = e
                r = rho[at] * depth
                glow = r * (w * lit + step * (t * (d * lit) + e))
                s = wd * inv * (0.5 * r)
                m = q * inv
                x = s * (lx - m * dx)
                y = s * (ly - m * dy)
                xs[k + 2, half(h), col(c)] = x
                ys[k, half(h), col(c)] = y
                zs[k, half(h), col(c)] = s * (lz - m * dz)
                parts[k + 1, half(h), col(c)] = glow
                parts[k, half(h), col(c)] += xs[k, half(h), col(c)] - x
                outermost.append(y[7 * h : 7 * h + 1])
            top, bottom = outermost
            row_one[k, :, col(c)] = jnp.where(row_first, bottom, top)
            row_two[k, :, col(c)] = jnp.where(row_first, top, bottom)

    copies = []

    def send(source, target, start, count, sem):
        at = pl.ds(start, count)
        copies.append(pltpu.make_async_copy(source.at[at], target.at[at], sem))
        copies[-1].start()

    arrivals[0].wait()
    for b in range(blocks):
        if b < blocks - 1:
            arrivals[b + 1].wait()
        pl.loop(b * BLOCK, (b + 1) * BLOCK, unroll=4)(layer)
        send(ys, adj_y, b * BLOCK, BLOCK, y_sems.at[b])
        send(zs, adj_z, b * BLOCK, BLOCK, z_sems.at[b])
    for c in range(nc):
        for h in range(2):
            at = (half(h), col(c))
            parts[ndep, half(h), col(c)] += xs[ndep, half(h), col(c)]
            first_x = xs[2, half(h), col(c)]
            last_x = xs[ndep + 1, half(h), col(c)] / ends[0, half(h), col(c)]
            to_near[at] = jnp.where(core_first, last_x, first_x)
            to_cross[at] = jnp.where(core_first, first_x, last_x)
    for copy in copies:
        copy.wait()


def scan_kernel(packed, out):
    slabs = packed.shape[0]
    front = jnp.ones((1, 384), jnp.float32)
    weighed = []
    for m in range(slabs):
        out[m, :, 0:384] = front
        weighed.append(front[:, :256] * packed[m, :, 384:640])
        front = front * packed[m, :, 0:384]
    behind = jnp.zeros((1, 256), jnp.float32)
    for m in reversed(range(slabs)):
        out[m, :, 384:640] = behind
        behind = behind + weighed[m]


def combine_kernel(
    step, depth, place, scanned, x_near, x_cross, y_one, y_two, rho, ends, parts, adj_y, adj_z,
    out, front, base, edge, ys, zs, buf, y_sems, z_sems, out_sems,
):
    ndep, _, ncol = out.shape
    nc = ncol // LANES
    first, last, head, tail = ids()
    outer, beyond = facing(place, x_near, x_cross, y_one, y_two)
    spans = list(zip(CUTS[:-1], CUTS[1:]))
    arrivals = []
    for b, (start, stop) in enumerate(spans):
        at = pl.ds(start, stop - start)
        arrivals.append(
            [
                pltpu.make_async_copy(source.at[at], target.at[at], sems.at[b])
                for source, target, sems in ((adj_y, ys, y_sems), (adj_z, zs, z_sems))
            ]
        )
        for copy in arrivals[-1]:
            copy.start()
    for c in range(nc):
        for a in range(8):
            p = a * nc + c
            front[2 * a : 2 * a + 1, col(c)] = scanned[p, :, 0:128]
            front[2 * a + 1 : 2 * a + 2, col(c)] = scanned[p, :, 128:256]
            base[2 * a : 2 * a + 1, col(c)] = scanned[p, :, 384:512]
            base[2 * a + 1 : 2 * a + 2, col(c)] = scanned[p, :, 512:640]
        edge[0, :, col(c)] = scanned[c, :, 256:384]
        edge[1, :, col(c)] = scanned[7 * nc + c, :, 256:384]
    for c in range(nc):
        for h in range(2):
            at = (half(h), col(c))
            base[at] = (depth * step) * (base[at] + front[at] * (rho[at] * ends[1, half(h), col(c)]))

    def layer(k):
        zt, yt = [[], []], [[], []]
        for h in range(2):
            for c in range(nc):
                f = front[half(h), col(c)]
                zt[h].append(f * zs[k, half(h), col(c)])
                yt[h].append(f * ys[k, half(h), col(c)])
        zn = [col_neighbours(zt[h], first, last) for h in range(2)]
        for c in range(nc):
            lo = wide(edge[0, :, col(c)] * beyond(k, c, True))
            hi = wide(edge[1, :, col(c)] * beyond(k, c, False))
            yn = row_neighbours(yt[0][c], yt[1][c], lo, hi, head, tail)
            for h in range(2):
                at, cell = (half(h), col(c)), (k, half(h), col(c))
                own = parts[k + 1, half(h), col(c)]
                buf[cell] = (front[at] * own - base[at]) + (
                    (yn[0][h] - yn[1][h]) + (zn[h][0][c] - zn[h][1][c])
                )

    copies = []
    for b, (start, stop) in enumerate(spans):
        for copy in arrivals[b]:
            copy.wait()
        pl.loop(start, stop, unroll=stop - start)(layer)
        for c in range(nc):
            for h in range(2):
                at = (half(h), col(c))
                if b == 0:
                    buf[0, half(h), col(c)] += front[at] * outer(at, True)
                if stop == ndep:
                    x = outer(at, False) * ends[0, half(h), col(c)]
                    buf[ndep - 1, half(h), col(c)] -= front[at] * x
        at = pl.ds(start, stop - start)
        copies.append(pltpu.make_async_copy(buf.at[at], out.at[at], out_sems.at[b]))
        copies[-1].start()
    for copy in copies:
        copy.wait()


def params(mib):
    return pltpu.CompilerParams(vmem_limit_bytes=mib << 20)


def cost(flops, nbytes):
    return pl.CostEstimate(flops=flops, bytes_accessed=nbytes, transcendentals=0)


def near_memory(*arrays):
    return [pltpu.with_memory_space_constraint(a, pltpu.VMEM) for a in arrays]


def far_memory(*arrays):
    return [pltpu.with_memory_space_constraint(a, pltpu.HBM) for a in arrays]


def local(density, light_dir, colour_tint, cotangent):
    ndep, nrow, ncol = density.shape
    slabs = lax.axis_size(RAY)
    rows = lax.axis_size("row")
    full_depth = float(ndep * slabs)
    step = EXTINCTION / full_depth
    place = jnp.stack([lax.axis_index(RAY[2]), lax.axis_index("row") % 2]).astype(jnp.int32)

    def pairs(start, stop):
        return [(i + n, i + 1 - n) for i in range(start, stop - 1, 2) for n in range(2)]

    def exchange(row_one, row_two, to_near, to_cross):
        return near_memory(
            lax.ppermute(to_near, RAY[2], pairs(0, 2)),
            lax.ppermute(to_cross, RAY, pairs(1, slabs)),
            lax.ppermute(row_one, "row", pairs(0, rows)),
            lax.ppermute(row_two, "row", pairs(1, rows)),
        )

    def vmem(*shape):
        return pltpu.VMEM(shape, jnp.float32)

    def hbm(*shape):
        return pltpu.HBM(shape, jnp.float32)

    cube, layer, rim = (ndep, nrow, ncol), (nrow, ncol), (ndep, 1, ncol)
    share, summed = (slabs, 1, 5 * LANES), (ndep + 1, 1, ncol)
    blocks = ndep // BLOCK
    cells = ndep * nrow * ncol
    sem = pltpu.SemaphoreType.DMA
    held, held_cot, *pieces = pl.pallas_call(
        gather_kernel,
        out_shape=(vmem(*cube), vmem(*cotangent.shape), vmem(*summed), vmem(*summed), vmem(*layer), vmem(*layer)),
        in_specs=[SM, HBM, HBM],
        out_specs=[VM] * 6,
        scratch_shapes=[sem((ndep // PIECE,)), sem],
        compiler_params=params(4),
        name="gather",
    )(place, *far_memory(density, cotangent))
    halos = exchange(*pieces)
    inner = pl.pallas_call(
        functools.partial(inner_kernel, step),
        out_shape=(vmem(*cube),) * 3 + (vmem(2, *layer),),
        in_specs=[SM, VM],
        out_specs=[VM] * 4,
        compiler_params=params(4),
        cost_estimate=cost(50 * cells, 16 * cells),
        name="inner",
    )(light_dir, held)
    packed, ends, rho = pl.pallas_call(
        functools.partial(forward_kernel, step),
        out_shape=(vmem(*share), vmem(2, *layer), vmem(*layer)),
        in_specs=[SM, SM, SM] + [VM] * 10,
        out_specs=[VM] * 3,
        scratch_shapes=[vmem(*layer)],
        compiler_params=params(4),
        cost_estimate=cost(30 * cells, 4 * cells),
        name="forward",
    )(place, light_dir, colour_tint, held, held_cot, *inner, *halos)

    scanned = lax.all_to_all(packed, RAY, 0, 0)
    part, adj_y, adj_z, to_near, to_cross, row_one, row_two = pl.pallas_call(
        functools.partial(adjoint_kernel, step, full_depth),
        out_shape=(vmem(ndep + 1, nrow, ncol), hbm(*cube), hbm(*cube))
        + (vmem(*layer), vmem(*layer), vmem(*rim), vmem(*rim)),
        in_specs=[SM, SM, HBM] + [VM] * 6,
        out_specs=[VM, HBM, HBM] + [VM] * 4,
        scratch_shapes=[
            vmem(ndep + 2, nrow, ncol),
            vmem(ndep + 2, nrow, ncol),
            vmem(*cube),
            vmem(*cube),
            vmem(*layer),
            vmem(*layer),
            sem((blocks,)),
            sem((blocks,)),
            sem((blocks,)),
        ],
        compiler_params=params(16),
        cost_estimate=cost(70 * cells, 16 * cells),
        name="adjoint",
    )(place, light_dir, *far_memory(density), *halos, rho, ends)
    scanned, to_near, to_cross, row_one, row_two = lax.optimization_barrier(
        (scanned, to_near, to_cross, row_one, row_two)
    )
    scanned = pl.pallas_call(
        scan_kernel,
        out_shape=vmem(*share),
        in_specs=[VM],
        out_specs=VM,
        compiler_params=params(4),
        name="scan",
    )(*near_memory(scanned))
    scanned = lax.all_to_all(scanned, RAY, 0, 0)
    rims = exchange(row_one, row_two, to_near, to_cross)
    return pl.pallas_call(
        functools.partial(combine_kernel, step, full_depth),
        out_shape=sds(*cube),
        in_specs=[SM] + [VM] * 8 + [HBM] * 2,
        out_specs=HBM,
        scratch_shapes=[
            vmem(*layer),
            vmem(*layer),
            vmem(2, 1, ncol),
            vmem(*cube),
            vmem(*cube),
            vmem(*cube),
            sem((len(CUTS),)),
            sem((len(CUTS),)),
            sem((len(CUTS),)),
        ],
        compiler_params=params(16),
        cost_estimate=cost(12 * cells, 16 * cells),
        name="combine",
    )(place, *near_memory(scanned), *rims, rho, ends, part, *far_memory(adj_y, adj_z))


def solution(mesh):
    torus = Mesh(
        mesh.devices.reshape(4, 8, 2, mesh.shape["row"]), ("ray_0", "ray_1", "ray_2", "row")
    )
    placed = (P(RAY, "row", None), P(), P(), P(None, "row", None))
    return jax.shard_map(
        local, mesh=torus, in_specs=placed, out_specs=P(RAY, "row", None), check_vma=False
    )
```
